32 devices in a mesh: fsdp: 16 (over z, y, x), replica: 2 (over core).
Axes of the slice: x: 2, y: 2, z: 4, core: 2. Of those that a mesh axis runs over, the one named last changes fastest.
Arguments:
- tokens: bfloat16 [4352, 1024], P(('fsdp', 'replica')), may hold values from -6 to 6
- cotangent: bfloat16 [4352, 1024], P(('fsdp', 'replica')), may hold values from -6 to 6
- w_in: bfloat16 [1024, 3072], P('fsdp'), may hold values from -0.1875 to 0.1875
- w_out: bfloat16 [1024, 1024], P('fsdp'), may hold values from -0.1875 to 0.1875
- w_gate: bfloat16 [1024, 4608], P('fsdp'), may hold values from -0.1875 to 0.1875
- w_up: bfloat16 [1024, 4608], P('fsdp'), may hold values from -0.1875 to 0.1875
- w_down: bfloat16 [4608, 1024], P('fsdp'), may hold values from -0.09375 to 0.09375
- norm1_scale: float32 [1024], replicated, may hold values from 0.5 to 1.5
- norm2_scale: float32 [1024], replicated, may hold values from 0.5 to 1.5
- conv_weight: float32 [3, 1024], replicated, may hold values from -3 to 3
- dev_extra: int32 [32], replicated, may hold values from 1 to 134, 4032 in all
- seq_lengths: int32 [6], replicated, may hold values from 1 to 1024, 4096 in all
Outputs:
- block_out: bfloat16 [4352, 1024], P(('fsdp', 'replica'))
- d_tokens: bfloat16 [4352, 1024], P(('fsdp', 'replica'))
- d_w_in: float32 [1024, 3072], P('fsdp')
- d_w_out: float32 [1024, 1024], P('fsdp')
- d_w_gate: float32 [1024, 4608], P('fsdp')
- d_w_up: float32 [1024, 4608], P('fsdp')
- d_w_down: float32 [4608, 1024], P('fsdp')
- d_norm1: float32 [1024], replicated
- d_norm2: float32 [1024], replicated
- d_conv: float32 [3, 1024], replicated
The draws below stay inside these ranges and needn't reach their ends.
Inputs may be any that keep to these rules, and one draw needn't show every extreme that they name: Device d holds dev_extra[d] + 2 consecutive packed tokens in its first rows, devices in the order of fsdp+replica, the rest of its 136 rows are padding; some device is full in every draw. `seq_lengths`: the sequences are packed back to back in this order over all tokens, one of them exactly 1024 long.
All inputs are finite; a program needn't handle non-finite values.
Results may differ from the reference program's by a relative error of at most 0.011.
Values may be sent and summed in bfloat16 or wider, within the bound.
A program may use at most 320 MiB of HBM per device.

```python
import math
import jax
import jax.numpy as jnp
import numpy as np
from jax import lax

D = 1024
FF = 4608
ROWS_DEV = 136
SEQ_MAX = 1024
TOK_DEV = 128
ROWS = 4352
TOTAL = 4096
NSEQ = 6
DEVICES = 32


def level_of(key, dims, shards, smallest, top_value):
    gain, own = 1.0, jax.random.fold_in(key, 6)
    for dim, blocks in shards:
        heights = jnp.exp(jax.random.uniform(jax.random.fold_in(own, dim), (blocks,), jnp.float32, smallest / len(shards), top_value / len(shards)))
        gain = gain * jnp.repeat(heights, dims[dim] // blocks).reshape([-1 if axis == dim else 1 for axis in range(len(dims))])
    return gain


def profile(count, total, reach, skew):
    weights = [(1 << 20) // math.isqrt(rank ** skew) + 1 for rank in range(2, count + 1)]
    rest, holding = total - reach - (count - 1), [1] * (count - 1)
    while rest > 0:
        movable = [i for i in range(count - 1) if holding[i] < reach]
        whole, remaining = sum([weights[i] for i in movable]), rest
        for i in movable:
            addition = min(reach - holding[i], max(1, remaining * weights[i] // whole), rest)
            holding[i] = holding[i] + addition
            rest = rest - addition
    return np.array([reach] + holding)


def ragged_sizes(rng, count, total, most, skew):
    if count == 2:
        one = jax.random.randint(rng, (), max(1, total - most), min(most, total - 1) + 1)
        return jnp.stack([one, total - one])
    lengths = jnp.asarray(profile(count, total, most, skew), jnp.int32)
    twos = (count - 1) // 2
    giver, receiver = lengths[1:1 + 2 * twos:2], lengths[2:2 + 2 * twos:2]
    room = jnp.minimum(giver - 1, most - receiver)
    moved = jax.random.randint(jax.random.fold_in(rng, 1), (twos,), 0, 1 << 20) % (room + 1)
    lengths = lengths.at[1:1 + 2 * twos:2].set(giver - moved).at[2:2 + 2 * twos:2].set(receiver + moved)
    return lengths[jax.random.permutation(jax.random.fold_in(rng, 2), count)]


def normal_values(stream_key, extent, spread, most, pieces=(), kind=jnp.bfloat16):
    array = spread * jax.random.normal(stream_key, extent, jnp.float32)
    if pieces:
        array = array * level_of(stream_key, extent, pieces, -0.22, 0.18)
    return jnp.clip(array, -most, most).astype(kind)


def setup_inputs(seed: int = 0) -> dict:
    arg_keys = jax.random.split(jax.random.key(seed), 13)
    return {
        "tokens": normal_values(arg_keys[0], (ROWS, D), 1.0, 6.0, ((0, 32),)),
        "cotangent": normal_values(arg_keys[1], (ROWS, D), 1.0, 6.0, ((0, 32),)),
        "w_in": normal_values(arg_keys[2], (D, 3 * D), D ** -0.5, 0.1875, ((0, 16),)),
        "w_out": normal_values(arg_keys[3], (D, D), D ** -0.5, 0.1875, ((0, 16),)),
        "w_gate": normal_values(arg_keys[4], (D, FF), D ** -0.5, 0.1875, ((0, 16),)),
        "w_up": normal_values(arg_keys[5], (D, FF), D ** -0.5, 0.1875, ((0, 16),)),
        "w_down": normal_values(arg_keys[6], (FF, D), FF ** -0.5, 0.09375, ((0, 16),)),
        "norm1_scale": jnp.clip(1.0 + 0.1 * jax.random.normal(arg_keys[7], (D,), jnp.float32), 0.5, 1.5),
        "norm2_scale": jnp.clip(1.0 + 0.1 * jax.random.normal(arg_keys[8], (D,), jnp.float32), 0.5, 1.5),
        "conv_weight": normal_values(arg_keys[9], (3, D), 0.6, 3.0, (), jnp.float32),
        "dev_extra": ragged_sizes(arg_keys[10], DEVICES, DEVICES * (TOK_DEV - 2), ROWS_DEV - 2, 2).astype(jnp.int32),
        "seq_lengths": ragged_sizes(arg_keys[11], NSEQ, TOTAL, SEQ_MAX, 1).astype(jnp.int32),
    }


epsilon = 1e-05
exact_mode = lax.Precision.HIGHEST

@jax.custom_vjp
def low(v):
    return lax.optimization_barrier(v.astype(jnp.bfloat16)).astype(jnp.float32)

@jax.custom_vjp
def low_back(v):
    return v

def low_keep(v):
    return (low(v), None)

def low_pass(kept, grad):
    return (grad,)

def back_keep(v):
    return (v, None)

def back_low(kept, grad):
    return (low(grad),)
low.defvjp(low_keep, low_pass)
low_back.defvjp(back_keep, back_low)

def matmul(left, right):
    return jnp.dot(left, right, precision=exact_mode, preferred_element_type=jnp.float32)

def rms_scale(v):
    return lax.rsqrt(lax.optimization_barrier(jnp.mean(v * v, axis=-1, keepdims=True)) + epsilon)

def reference(tokens, cotangent, w_in, w_out, w_gate, w_up, w_down, norm1_scale, norm2_scale, conv_weight, dev_extra, seq_lengths):
    counts = (dev_extra + 2).astype(jnp.int32)
    end_rows = jnp.cumsum(counts).astype(jnp.int32)
    offsets = (end_rows - counts).astype(jnp.int32)
    packed = jnp.arange(TOTAL, dtype=jnp.int32)
    owner_dev = lax.optimization_barrier(jnp.sum((packed[:, None] >= end_rows[None, :]).astype(jnp.int32), axis=1)).astype(jnp.int32)
    slot_row = (owner_dev * ROWS_DEV + packed - offsets[owner_dev]).astype(jnp.int32)
    seq_first = (jnp.cumsum(seq_lengths) - seq_lengths).astype(jnp.int32)
    is_start = jnp.any(packed[:, None] == seq_first[None, :], axis=1)
    keep_one = 1.0 - is_start.astype(jnp.float32)
    keep_two = keep_one * jnp.concatenate([jnp.zeros((1,), jnp.float32), keep_one[:-1]])
    inputs = tokens.astype(jnp.float32)[slot_row]
    grad_out = cotangent.astype(jnp.float32)[slot_row]
    block_rows = TOTAL // 8

    def forward(x, weight_in, weight_out, weight_gate, weight_up, weight_down, scale_one, scale_two, kernel):

        def section_in(rows_x):
            normed_in = low(rows_x * rms_scale(rows_x) * scale_one)
            return low(low_back(matmul(normed_in, weight_in)))
        in_proj = lax.map(jax.checkpoint(section_in), x.reshape(8, block_rows, D)).reshape(TOTAL, 3 * D)
        b_part = in_proj[:, :D]
        c_part = in_proj[:, D:2 * D]
        x_part = in_proj[:, 2 * D:]
        u = b_part * x_part
        u_prev = jnp.concatenate([jnp.zeros((1, D), jnp.float32), u[:-1]], axis=0) * keep_one[:, None]
        u_prev2 = jnp.concatenate([jnp.zeros((2, D), jnp.float32), u[:-2]], axis=0) * keep_two[:, None]
        v = kernel[2] * u + kernel[1] * u_prev + kernel[0] * u_prev2
        y_val = low(c_part * v)

        def section_out(pair):
            rows_x, rows_y = pair
            hidden_res = rows_x + low_back(matmul(rows_y, weight_out))
            normed_ffn = low(hidden_res * rms_scale(hidden_res) * scale_two)
            gate_val = low_back(matmul(normed_ffn, weight_gate))
            up_val = low_back(matmul(normed_ffn, weight_up))
            act_val = low(jax.nn.silu(gate_val) * up_val)
            return hidden_res + matmul(act_val, weight_down)
        result = lax.map(jax.checkpoint(section_out), (x.reshape(8, block_rows, D), y_val.reshape(8, block_rows, D)))
        return result.reshape(TOTAL, D)
    primals = (inputs, w_in.astype(jnp.float32), w_out.astype(jnp.float32), w_gate.astype(jnp.float32), w_up.astype(jnp.float32), w_down.astype(jnp.float32), norm1_scale.astype(jnp.float32), norm2_scale.astype(jnp.float32), conv_weight.astype(jnp.float32))
    result, pullback = jax.vjp(forward, *primals)
    grads = pullback(grad_out)

    def unpack(values):
        return jnp.zeros((ROWS, D), jnp.float32).at[slot_row].set(values).astype(jnp.bfloat16)
    return (unpack(result), unpack(grads[0]), grads[1], grads[2], grads[3], grads[4], grads[5], grads[6], grads[7], grads[8])
```

```python
import jax
import jax.numpy as jnp
from jax import lax
from jax.sharding import PartitionSpec as P

epsilon = 1e-05


def passed_along(block, axis, distance):
    devices = range(lax.axis_size(axis))
    route = [(i - distance, i) for i in devices if i - distance in devices]
    return lax.ppermute(block, axis, route)


def rms_scale(v):
    return lax.rsqrt(jnp.mean(v * v, axis=-1, keepdims=True) + epsilon)


def product(left, right):
    return jnp.dot(left, right, preferred_element_type=jnp.float32)


def product_left(left, right):
    return lax.dot_general(
        left, right, (((0,), (0,)), ((), ())), preferred_element_type=jnp.float32
    )


def product_right(left, right):
    return lax.dot_general(
        left, right, (((1,), (1,)), ((), ())), preferred_element_type=jnp.float32
    )


def scattered_sum(value):
    return lax.psum_scatter(
        value.astype(jnp.bfloat16), "fsdp", scatter_dimension=0, tiled=True
    ).astype(jnp.float32)


def norm_back(grad, scaled, scale, gain):
    grad_gain = grad * gain
    return scale * (grad_gain - scaled * jnp.mean(grad_gain * scaled, axis=-1, keepdims=True))


def body(
    tokens,
    cotangent,
    w_in,
    w_out,
    w_gate,
    w_up,
    w_down,
    norm1_scale,
    norm2_scale,
    conv_weight,
    dev_extra,
    seq_lengths,
):
    rows_dev = tokens.shape[0]
    width = tokens.shape[1]
    hidden = w_gate.shape[1]
    group = lax.axis_size("fsdp")
    part = w_down.shape[0]
    whole_in = lax.all_gather(w_in, "fsdp", axis=0, tiled=True)
    whole_out = lax.all_gather(w_out, "fsdp", axis=0, tiled=True)
    own_rows = w_gate.shape[0]
    pair = jnp.concatenate(
        [w_gate.reshape(own_rows, group, part), w_up.reshape(own_rows, group, part)], axis=2
    )
    pair = lax.all_to_all(
        pair.transpose(1, 0, 2), "fsdp", split_axis=0, concat_axis=0, tiled=True
    ).reshape(width, 2 * part)
    device = lax.axis_index(("fsdp", "replica"))
    counts = dev_extra + 2
    end_rows = jnp.cumsum(counts)
    device_ids = jnp.arange(counts.shape[0], dtype=jnp.int32)
    mine = device_ids == device
    count = jnp.sum(jnp.where(mine, counts, 0))
    offset = jnp.sum(jnp.where(mine, end_rows, 0)) - count
    row_ids = jnp.arange(rows_dev, dtype=jnp.int32)
    valid = row_ids < count
    position = offset + row_ids
    seq_first = jnp.cumsum(seq_lengths) - seq_lengths
    is_start = jnp.any(position[:, None] == seq_first[None, :], axis=1)
    prev_start = jnp.any((position - 1)[:, None] == seq_first[None, :], axis=1)
    keep_one = (valid & jnp.logical_not(is_start)).astype(jnp.float32)[:, None]
    keep_two = keep_one * jnp.logical_not(prev_start).astype(jnp.float32)[:, None]
    inputs = tokens.astype(jnp.float32)
    scale_one = rms_scale(inputs)
    scaled_one = inputs * scale_one
    normed_in = (scaled_one * norm1_scale).astype(jnp.bfloat16)
    in_proj = product(normed_in, whole_in).astype(jnp.bfloat16)
    b_part = in_proj[:, :width]
    c_part = in_proj[:, width : 2 * width]
    x_part = in_proj[:, 2 * width :]
    rim_pair = (
        lax.dynamic_slice_in_dim(b_part, count - 2, 2, 0),
        lax.dynamic_slice_in_dim(x_part, count - 2, 2, 0),
    )
    rim = passed_along(jnp.concatenate(rim_pair, axis=0), ("fsdp", "replica"), 1)
    rim_b, rim_x = rim[:2], rim[2:]
    b_val = b_part.astype(jnp.float32)
    x_val = x_part.astype(jnp.float32)
    c_val = c_part.astype(jnp.float32)
    u = b_val * x_val
    u_ext = jnp.concatenate([rim_b.astype(jnp.float32) * rim_x.astype(jnp.float32), u], axis=0)
    u_prev = u_ext[1 : rows_dev + 1] * keep_one
    u_prev2 = u_ext[:rows_dev] * keep_two
    v = conv_weight[2] * u + conv_weight[1] * u_prev + conv_weight[0] * u_prev2
    y_val = (c_val * v).astype(jnp.bfloat16)
    hidden_res = inputs + product(y_val, whole_out)
    scale_two = rms_scale(hidden_res)
    scaled_two = hidden_res * scale_two
    normed_ffn = (scaled_two * norm2_scale).astype(jnp.bfloat16)
    grad_out = jnp.where(valid[:, None], cotangent, jnp.zeros_like(cotangent))
    grad_all = lax.all_gather(grad_out, "fsdp", axis=0, tiled=True)
    ffn_all = lax.all_gather(normed_ffn, "fsdp", axis=0, tiled=True)
    both = product(ffn_all, pair)
    gate_val, up_val = both[:, :part], both[:, part:]
    sigma = jax.nn.sigmoid(gate_val)
    silu_val = gate_val * sigma
    act_val = (silu_val * up_val).astype(jnp.bfloat16)
    grad_act = product_right(grad_all, w_down)
    grad_gate = (grad_act * up_val * sigma * (1.0 + gate_val * (1.0 - sigma))).astype(jnp.bfloat16)
    grad_up = (grad_act * silu_val).astype(jnp.bfloat16)
    grad_pair = jnp.concatenate([grad_gate, grad_up], axis=1)
    grad_ffn = scattered_sum(product_right(grad_pair, pair))
    result = hidden_res + scattered_sum(product(act_val, w_down))
    block_out = jnp.where(valid[:, None], result, 0.0).astype(jnp.bfloat16)
    gain_two = jnp.sum(grad_ffn * scaled_two, axis=0)
    grad_res = grad_out.astype(jnp.float32) + norm_back(
        grad_ffn, scaled_two, scale_two, norm2_scale
    )
    grad_mix = grad_res.astype(jnp.bfloat16)
    grad_y = product_right(grad_mix, whole_out)
    grad_c = grad_y * v
    grad_v = grad_y * c_val
    conv_grads = jnp.stack(
        [
            jnp.sum(grad_v * u_prev2, axis=0),
            jnp.sum(grad_v * u_prev, axis=0),
            jnp.sum(grad_v * u, axis=0),
        ]
    )
    term_one = conv_weight[1] * keep_one * grad_v
    term_two = conv_weight[0] * keep_two * grad_v
    grad_ext = (
        jnp.pad(term_two, ((0, 2), (0, 0)))
        + jnp.pad(term_one, ((1, 1), (0, 0)))
        + jnp.pad(conv_weight[2] * grad_v, ((2, 0), (0, 0)))
    )
    from_next = passed_along(grad_ext[:2], ("fsdp", "replica"), -1)
    grad_u = grad_ext[2:]
    grad_u = grad_u + lax.dynamic_update_slice_in_dim(
        jnp.zeros_like(grad_u), from_next, count - 2, 0
    )
    grad_proj = jnp.concatenate([grad_u * x_val, grad_c, grad_u * b_val], axis=1).astype(
        jnp.bfloat16
    )
    grad_norm_in = product_right(grad_proj, whole_in)
    gain_one = jnp.sum(grad_norm_in * scaled_one, axis=0)
    d_tokens = (grad_res + norm_back(grad_norm_in, scaled_one, scale_one, norm1_scale)).astype(
        jnp.bfloat16
    )
    small = lax.psum(
        jnp.concatenate([gain_one[None], gain_two[None], conv_grads], axis=0),
        ("fsdp", "replica"),
    )
    d_norm1, d_norm2, d_conv = small[0], small[1], small[2:]
    in_part = scattered_sum(product_left(normed_in, grad_proj))
    out_part = scattered_sum(product_left(y_val, grad_mix))
    pair_part = product_left(ffn_all, grad_pair).astype(jnp.bfloat16)
    pair_part = lax.all_to_all(
        pair_part.reshape(group, own_rows, 2 * part), "fsdp", split_axis=0, concat_axis=0, tiled=True
    )
    down_part = product_left(act_val, grad_all)
    in_part, out_part, pair_part, down_part = [
        value.astype(jnp.float32)
        for value in lax.psum(
            (
                in_part.astype(jnp.bfloat16),
                out_part.astype(jnp.bfloat16),
                pair_part,
                down_part.astype(jnp.bfloat16),
            ),
            "replica",
        )
    ]
    d_w_in = in_part
    d_w_out = out_part
    pair_part = pair_part.transpose(1, 0, 2)
    d_w_gate = pair_part[:, :, :part].reshape(own_rows, hidden)
    d_w_up = pair_part[:, :, part:].reshape(own_rows, hidden)
    return (
        block_out,
        d_tokens,
        d_w_in,
        d_w_out,
        d_w_gate,
        d_w_up,
        down_part,
        d_norm1,
        d_norm2,
        d_conv,
    )


def solution(mesh):
    placed = (
        P(("fsdp", "replica"), None),
        P(("fsdp", "replica"), None),
        P("fsdp", None),
        P("fsdp", None),
        P("fsdp", None),
        P("fsdp", None),
        P("fsdp", None),
        P(),
        P(),
        P(),
        P(),
        P(),
    )
    return jax.shard_map(
        body,
        mesh=mesh,
        in_specs=placed,
        out_specs=(
            P(("fsdp", "replica"), None),
            P(("fsdp", "replica"), None),
            P("fsdp", None),
            P("fsdp", None),
            P("fsdp", None),
            P("fsdp", None),
            P("fsdp", None),
            P(),
            P(),
            P(),
        ),
        check_vma=False,
    )
```

```python
import functools

import jax
import jax.numpy as jnp
from jax import lax
from jax.experimental import pallas as pl
from jax.experimental.pallas import tpu as pltpu
from jax.sharding import PartitionSpec as P

epsilon = 1e-05


class Place:
    def __init__(self, group):
        self.me = lax.axis_index("fsdp")
        self.core = lax.axis_index("replica")
        self.depth = group // 4
        self.mask_one = 1 + self.core
        self.mask_two = 2 - self.core
        self.bit_one = lax.rem(lax.div(self.me, self.mask_one), 2)
        self.bit_two = lax.rem(lax.div(self.me, self.mask_two), 2)
        self.z = lax.div(self.me, 4)

    def index(self, step, flip_one, flip_two):
        z = lax.rem(self.z + step, self.depth)
        one = 1 - self.bit_one if flip_one else self.bit_one
        two = 1 - self.bit_two if flip_two else self.bit_two
        return 4 * z + self.mask_one * one + self.mask_two * two

    def peers(self):
        line = [self.index(step, False, False) for step in range(1, self.depth)]
        return line + [self.index(0, True, False), self.index(0, False, True)]


def meet(place, sibling):
    barrier = pltpu.get_barrier_semaphore()
    peers = [{"fsdp": peer} for peer in place.peers()]
    if sibling:
        peers.append({"replica": 1 - place.core})
    for peer in peers:
        pl.semaphore_signal(barrier, inc=1, device_id=peer, device_id_type=pl.DeviceIdType.MESH)
    pl.semaphore_wait(barrier, len(peers))


def push(source, target, send, recv, peer):
    copy = pltpu.make_async_remote_copy(
        src_ref=source,
        dst_ref=target,
        send_sem=send,
        recv_sem=recv,
        device_id=peer,
        device_id_type=pl.DeviceIdType.MESH,
    )
    copy.start()
    return copy


def gather_kernel(group, sibling, x_ref, out_ref, local, sends, recvs):
    place = Place(group)
    depth = place.depth
    meet(place, sibling)
    half = out_ref.at[place.core] if sibling else out_ref
    one = {"fsdp": place.index(0, True, False)}
    two = {"fsdp": place.index(0, False, True)}
    first, second, shared = [], [], []

    def pass_on(source, number, to_one):
        row = place.index(-number % depth, not to_one, False)
        if to_one:
            at = depth - 1 + number
            first.append(push(source, half.at[row], sends.at[at], recvs.at[at], one))
        at = 2 * depth - 1 + len(second)
        second.append(push(source, half.at[row], sends.at[at], recvs.at[at], two))
        share(source, row)

    def share(source, row):
        if sibling:
            at = 4 * depth - 1 + len(shared)
            peer = {"replica": 1 - place.core}
            shared.append(push(source, half.at[row], sends.at[at], recvs.at[at], peer))

    keep = pltpu.make_async_copy(x_ref, half.at[place.me], local)
    keep.start()
    line = []
    for step in range(1, depth):
        peer = {"fsdp": place.index(step, False, False)}
        line.append(push(x_ref, half.at[place.me], sends.at[step - 1], recvs.at[step - 1], peer))
    pass_on(x_ref, 0, True)
    for step in range(1, depth):
        line[step - 1].wait_recv()
        pass_on(half.at[place.index(-step % depth, False, False)], step, True)
    for number in range(depth):
        first[number].wait_recv()
        pass_on(half.at[place.index(-number % depth, True, False)], number, False)
    for number in range(2 * depth):
        second[number].wait_recv()
        row = place.index(-number % depth, number >= depth, True)
        share(half.at[row], row)
    for copy in shared:
        copy.wait_recv()
    keep.wait()
    for copy in line + first + second + shared:
        copy.wait_send()


def gathered(block, number, sibling=False):
    group = lax.axis_size("fsdp")
    count = group - 1 + (group if sibling else 0)
    shape = (group,) + block.shape
    return pl.pallas_call(
        functools.partial(gather_kernel, group, sibling),
        out_shape=jax.ShapeDtypeStruct((2,) + shape if sibling else shape, block.dtype),
        in_specs=[pl.BlockSpec(memory_space=pl.ANY)],
        out_specs=pl.BlockSpec(memory_space=pl.ANY),
        scratch_shapes=[
            pltpu.SemaphoreType.DMA,
            pltpu.SemaphoreType.DMA((count,)),
            pltpu.SemaphoreType.DMA((count,)),
        ],
        compiler_params=pltpu.CompilerParams(collective_id=number, has_side_effects=True),
    )(block)


def sum_kernel(group, x_ref, out_ref, got_one, got_two, got_line, to_two, to_line, sends, recvs):
    place = Place(group)
    depth = place.depth
    meet(place, False)
    one = {"fsdp": place.index(0, True, False)}
    two = {"fsdp": place.index(0, False, True)}
    wide = jnp.float32
    first, second, line = [], [], []
    for flip in (True, False):
        for step in range(depth):
            at = len(first)
            block = x_ref.at[place.index(step + 1, True, flip)]
            first.append(push(block, got_one.at[at], sends.at[at], recvs.at[at], one))
    for step in range(depth):
        first[step].wait_recv()
        total = x_ref[place.index(step + 1, False, True)].astype(wide) + got_one[step].astype(wide)
        to_two[step] = total.astype(to_two.dtype)
        at = 2 * depth + step
        second.append(push(to_two.at[step], got_two.at[step], sends.at[at], recvs.at[at], two))
    for step in range(depth):
        first[depth + step].wait_recv()
        second[step].wait_recv()
        total = (
            x_ref[place.index(step + 1, False, False)].astype(wide)
            + got_one[depth + step].astype(wide)
            + got_two[step].astype(wide)
        )
        if step < depth - 1:
            to_line[step] = total.astype(to_line.dtype)
            at = 3 * depth + step
            peer = {"fsdp": place.index(step + 1, False, False)}
            line.append(push(to_line.at[step], got_line.at[step], sends.at[at], recvs.at[at], peer))
        else:
            out_ref[...] = total
    for step in range(depth - 1):
        line[step].wait_recv()
        out_ref[...] += got_line[step].astype(wide)
    for copy in first + second + line:
        copy.wait_send()


def sum_blocks(blocks, number):
    group = blocks.shape[0]
    depth = group // 4
    one = blocks.shape[1:]
    return pl.pallas_call(
        functools.partial(sum_kernel, group),
        out_shape=jax.ShapeDtypeStruct(one, jnp.float32),
        in_specs=[pl.BlockSpec(memory_space=pltpu.VMEM)],
        out_specs=pl.BlockSpec(memory_space=pltpu.VMEM),
        scratch_shapes=[
            pltpu.VMEM((2 * depth,) + one, blocks.dtype),
            pltpu.VMEM((depth,) + one, blocks.dtype),
            pltpu.VMEM((depth - 1,) + one, blocks.dtype),
            pltpu.VMEM((depth,) + one, blocks.dtype),
            pltpu.VMEM((depth - 1,) + one, blocks.dtype),
            pltpu.SemaphoreType.DMA((group - 1,)),
            pltpu.SemaphoreType.DMA((group - 1,)),
        ],
        compiler_params=pltpu.CompilerParams(
            collective_id=number, has_side_effects=True, vmem_limit_bytes=32 * 1024 * 1024
        ),
    )(blocks)


def own_kernels():
    return lax.axis_size("fsdp") == 16 and lax.axis_size("replica") == 2


def gather_rows(block, number):
    if not own_kernels():
        return lax.all_gather(block, "fsdp", axis=0, tiled=True)
    return gathered(block, number).reshape(-1, block.shape[1])


def other_core(value):
    return lax.ppermute(value, "replica", [(0, 1), (1, 0)])


def cores_sum(value):
    if lax.axis_size("replica") != 2:
        return lax.psum(value, "replica").astype(jnp.float32)
    return value.astype(jnp.float32) + other_core(value).astype(jnp.float32)


def mixer_sum(in_grad, out_grad):
    group = lax.axis_size("fsdp")
    both = jnp.concatenate([in_grad, out_grad], axis=1).astype(jnp.bfloat16)
    rows, columns = both.shape
    if not own_kernels():
        total = lax.psum_scatter(both, "fsdp", scatter_dimension=0, tiled=True)
        return cores_sum(total)
    core = lax.axis_index("replica")
    left, right = both[:, : columns // 2], both[:, columns // 2 :]
    mine = jnp.where(core == 0, left, right)
    theirs = other_core(jnp.where(core == 0, right, left))
    half = (mine.astype(jnp.float32) + theirs.astype(jnp.float32)).astype(jnp.bfloat16)
    half = sum_blocks(half.reshape(group, rows // group, columns // 2), 5)
    half = half.astype(jnp.bfloat16)
    back = other_core(half)
    return jnp.concatenate(
        [jnp.where(core == 0, half, back), jnp.where(core == 0, back, half)], axis=1
    ).astype(jnp.float32)


def passed_along(block, axis, distance):
    devices = range(lax.axis_size(axis))
    route = [(i - distance, i) for i in devices if i - distance in devices]
    return lax.ppermute(block, axis, route)


def rms_scale(v):
    return lax.rsqrt(jnp.mean(v * v, axis=-1, keepdims=True) + epsilon)


def product(left, right):
    return jnp.dot(left, right, preferred_element_type=jnp.float32)


def product_left(left, right):
    return lax.dot_general(
        left, right, (((0,), (0,)), ((), ())), preferred_element_type=jnp.float32
    )


def product_right(left, right):
    return lax.dot_general(
        left, right, (((1,), (1,)), ((), ())), preferred_element_type=jnp.float32
    )


def scattered_sum(value, number):
    value = value.astype(jnp.bfloat16)
    if not own_kernels():
        return lax.psum_scatter(value, "fsdp", scatter_dimension=0, tiled=True).astype(jnp.float32)
    group = lax.axis_size("fsdp")
    return sum_blocks(value.reshape(group, value.shape[0] // group, value.shape[1]), number)


def norm_back(grad, scaled, scale, gain):
    grad_gain = grad * gain
    return scale * (grad_gain - scaled * jnp.mean(grad_gain * scaled, axis=-1, keepdims=True))


def body(
    tokens,
    cotangent,
    w_in,
    w_out,
    w_gate,
    w_up,
    w_down,
    norm1_scale,
    norm2_scale,
    conv_weight,
    dev_extra,
    seq_lengths,
):
    rows_dev = tokens.shape[0]
    width = tokens.shape[1]
    hidden = w_gate.shape[1]
    group = lax.axis_size("fsdp")
    part = w_down.shape[0]
    if own_kernels():
        late = jnp.concatenate([w_in[:, 2 * width :], w_out], axis=1)
        chosen = jnp.where(lax.axis_index("replica") == 0, w_in[:, : 2 * width], late)
        halves = gathered(chosen, 0, sibling=True).reshape(2, width, 2 * width)
        whole_bc, whole_x, whole_out = halves[0], halves[1, :, :width], halves[1, :, width:]
    else:
        whole_in = lax.all_gather(w_in, "fsdp", axis=0, tiled=True)
        whole_bc, whole_x = whole_in[:, : 2 * width], whole_in[:, 2 * width :]
        whole_out = lax.all_gather(w_out, "fsdp", axis=0, tiled=True)
    own_rows = w_gate.shape[0]
    pair = jnp.concatenate(
        [w_gate.reshape(own_rows, group, part), w_up.reshape(own_rows, group, part)], axis=2
    )
    pair = lax.all_to_all(
        pair.transpose(1, 0, 2), "fsdp", split_axis=0, concat_axis=0, tiled=True
    ).reshape(width, 2 * part)
    device = lax.axis_index(("fsdp", "replica"))
    counts = dev_extra + 2
    end_rows = jnp.cumsum(counts)
    device_ids = jnp.arange(counts.shape[0], dtype=jnp.int32)
    mine = device_ids == device
    count = jnp.sum(jnp.where(mine, counts, 0))
    offset = jnp.sum(jnp.where(mine, end_rows, 0)) - count
    row_ids = jnp.arange(rows_dev, dtype=jnp.int32)
    valid = row_ids < count
    position = offset + row_ids
    seq_first = jnp.cumsum(seq_lengths) - seq_lengths
    is_start = jnp.any(position[:, None] == seq_first[None, :], axis=1)
    prev_start = jnp.any((position - 1)[:, None] == seq_first[None, :], axis=1)
    keep_one = (valid & jnp.logical_not(is_start)).astype(jnp.float32)[:, None]
    keep_two = keep_one * jnp.logical_not(prev_start).astype(jnp.float32)[:, None]
    inputs = tokens.astype(jnp.float32)
    scale_one = rms_scale(inputs)
    scaled_one = inputs * scale_one
    normed_in = (scaled_one * norm1_scale).astype(jnp.bfloat16)
    bc_part = product(normed_in, whole_bc).astype(jnp.bfloat16)
    b_part = bc_part[:, :width]
    c_part = bc_part[:, width:]
    x_part = product(normed_in, whole_x).astype(jnp.bfloat16)
    rim_pair = (
        lax.dynamic_slice_in_dim(b_part, count - 2, 2, 0),
        lax.dynamic_slice_in_dim(x_part, count - 2, 2, 0),
    )
    rim = passed_along(jnp.concatenate(rim_pair, axis=0), ("fsdp", "replica"), 1)
    rim_b, rim_x = rim[:2], rim[2:]
    b_val = b_part.astype(jnp.float32)
    x_val = x_part.astype(jnp.float32)
    c_val = c_part.astype(jnp.float32)
    u = b_val * x_val
    u_ext = jnp.concatenate([rim_b.astype(jnp.float32) * rim_x.astype(jnp.float32), u], axis=0)
    u_prev = u_ext[1 : rows_dev + 1] * keep_one
    u_prev2 = u_ext[:rows_dev] * keep_two
    v = conv_weight[2] * u + conv_weight[1] * u_prev + conv_weight[0] * u_prev2
    y_val = (c_val * v).astype(jnp.bfloat16)
    hidden_res = inputs + product(y_val, whole_out)
    scale_two = rms_scale(hidden_res)
    scaled_two = hidden_res * scale_two
    normed_ffn = (scaled_two * norm2_scale).astype(jnp.bfloat16)
    grad_out = jnp.where(valid[:, None], cotangent, jnp.zeros_like(cotangent))
    grad_all = gather_rows(grad_out, 1)
    ffn_all = gather_rows(normed_ffn, 2)
    both = product(ffn_all, pair)
    gate_val, up_val = both[:, :part], both[:, part:]
    sigma = jax.nn.sigmoid(gate_val)
    silu_val = gate_val * sigma
    act_val = (silu_val * up_val).astype(jnp.bfloat16)
    grad_act = product_right(grad_all, w_down)
    grad_gate = (grad_act * up_val * sigma * (1.0 + gate_val * (1.0 - sigma))).astype(jnp.bfloat16)
    grad_up = (grad_act * silu_val).astype(jnp.bfloat16)
    grad_pair = jnp.concatenate([grad_gate, grad_up], axis=1)
    grad_ffn = scattered_sum(product_right(grad_pair, pair), 3)
    result = hidden_res + scattered_sum(product(act_val, w_down), 4)
    block_out = jnp.where(valid[:, None], result, 0.0).astype(jnp.bfloat16)
    gain_two = jnp.sum(grad_ffn * scaled_two, axis=0)
    grad_res = grad_out.astype(jnp.float32) + norm_back(
        grad_ffn, scaled_two, scale_two, norm2_scale
    )
    grad_mix = grad_res.astype(jnp.bfloat16)
    grad_y = product_right(grad_mix, whole_out)
    grad_c = grad_y * v
    grad_v = grad_y * c_val
    conv_grads = jnp.stack(
        [
            jnp.sum(grad_v * u_prev2, axis=0),
            jnp.sum(grad_v * u_prev, axis=0),
            jnp.sum(grad_v * u, axis=0),
        ]
    )
    term_one = conv_weight[1] * keep_one * grad_v
    term_two = conv_weight[0] * keep_two * grad_v
    grad_ext = (
        jnp.pad(term_two, ((0, 2), (0, 0)))
        + jnp.pad(term_one, ((1, 1), (0, 0)))
        + jnp.pad(conv_weight[2] * grad_v, ((2, 0), (0, 0)))
    )
    from_next = passed_along(grad_ext[:2], ("fsdp", "replica"), -1)
    grad_u = grad_ext[2:]
    grad_u = grad_u + lax.dynamic_update_slice_in_dim(
        jnp.zeros_like(grad_u), from_next, count - 2, 0
    )
    grad_proj = jnp.concatenate([grad_u * x_val, grad_c, grad_u * b_val], axis=1).astype(
        jnp.bfloat16
    )
    grad_norm_in = product_right(grad_proj[:, : 2 * width], whole_bc) + product_right(
        grad_proj[:, 2 * width :], whole_x
    )
    gain_one = jnp.sum(grad_norm_in * scaled_one, axis=0)
    d_tokens = (grad_res + norm_back(grad_norm_in, scaled_one, scale_one, norm1_scale)).astype(
        jnp.bfloat16
    )
    small = lax.psum(
        jnp.concatenate([gain_one[None], gain_two[None], conv_grads], axis=0),
        ("fsdp", "replica"),
    )
    d_norm1, d_norm2, d_conv = small[0], small[1], small[2:]
    mix_part = mixer_sum(product_left(normed_in, grad_proj), product_left(y_val, grad_mix))
    pair_part = product_left(ffn_all, grad_pair).astype(jnp.bfloat16)
    pair_part = lax.all_to_all(
        pair_part.reshape(group, own_rows, 2 * part), "fsdp", split_axis=0, concat_axis=0, tiled=True
    )
    down_part = product_left(act_val, grad_all)
    pair_part = cores_sum(pair_part)
    down_part = cores_sum(down_part.astype(jnp.bfloat16))
    d_w_in = mix_part[:, : 3 * width]
    d_w_out = mix_part[:, 3 * width :]
    pair_part = pair_part.transpose(1, 0, 2)
    d_w_gate = pair_part[:, :, :part].reshape(own_rows, hidden)
    d_w_up = pair_part[:, :, part:].reshape(own_rows, hidden)
    return (
        block_out,
        d_tokens,
        d_w_in,
        d_w_out,
        d_w_gate,
        d_w_up,
        down_part,
        d_norm1,
        d_norm2,
        d_conv,
    )


def solution(mesh):
    placed = (
        P(("fsdp", "replica"), None),
        P(("fsdp", "replica"), None),
        P("fsdp", None),
        P("fsdp", None),
        P("fsdp", None),
        P("fsdp", None),
        P("fsdp", None),
        P(),
        P(),
        P(),
        P(),
        P(),
    )
    return jax.shard_map(
        body,
        mesh=mesh,
        in_specs=placed,
        out_specs=(
            P(("fsdp", "replica"), None),
            P(("fsdp", "replica"), None),
            P("fsdp", None),
            P("fsdp", None),
            P("fsdp", None),
            P("fsdp", None),
            P("fsdp", None),
            P(),
            P(),
            P(),
        ),
        check_vma=False,
    )
```

```python
import functools

import jax
import jax.numpy as jnp
from jax import lax
from jax.experimental import pallas as pl
from jax.experimental.pallas import tpu as pltpu
from jax.sharding import PartitionSpec as P

epsilon = 1e-05


class Place:
    def __init__(self, group):
        self.me = lax.axis_index("fsdp")
        self.core = lax.axis_index("replica")
        self.depth = group // 4
        self.mask_one = 1 + self.core
        self.mask_two = 2 - self.core
        self.bit_one = lax.rem(lax.div(self.me, self.mask_one), 2)
        self.bit_two = lax.rem(lax.div(self.me, self.mask_two), 2)
        self.z = lax.div(self.me, 4)

    def index(self, step, flip_one, flip_two):
        z = lax.rem(self.z + step, self.depth)
        one = 1 - self.bit_one if flip_one else self.bit_one
        two = 1 - self.bit_two if flip_two else self.bit_two
        return 4 * z + self.mask_one * one + self.mask_two * two

    def peers(self):
        line = [self.index(step, False, False) for step in range(1, self.depth)]
        return line + [self.index(0, True, False), self.index(0, False, True)]


def meet(place, sibling):
    barrier = pltpu.get_barrier_semaphore()
    peers = [{"fsdp": peer} for peer in place.peers()]
    if sibling:
        peers.append({"replica": 1 - place.core})
    for peer in peers:
        pl.semaphore_signal(barrier, inc=1, device_id=peer, device_id_type=pl.DeviceIdType.MESH)
    pl.semaphore_wait(barrier, len(peers))


def push(source, target, send, recv, peer):
    copy = pltpu.make_async_remote_copy(
        src_ref=source,
        dst_ref=target,
        send_sem=send,
        recv_sem=recv,
        device_id=peer,
        device_id_type=pl.DeviceIdType.MESH,
    )
    copy.start()
    return copy


def gather_kernel(group, shares, *refs):
    count = len(shares)
    x_refs, outs = refs[:count], refs[count : 2 * count]
    local, sends, recvs = refs[2 * count :]
    place = Place(group)
    depth = place.depth
    meet(place, any(shares))
    halves = [out.at[place.core] if share else out for out, share in zip(outs, shares)]
    one = {"fsdp": place.index(0, True, False)}
    two = {"fsdp": place.index(0, False, True)}
    lanes = range(count)
    line, first, second, shared = [[[] for _ in lanes] for _ in range(4)]

    def pass_on(lane, source, number, to_one):
        half = halves[lane]
        row = place.index(-number % depth, not to_one, False)
        if to_one:
            at = depth - 1 + number
            sems = sends.at[lane, at], recvs.at[lane, at]
            first[lane].append(push(source, half.at[row], *sems, one))
        at = 2 * depth - 1 + len(second[lane])
        sems = sends.at[lane, at], recvs.at[lane, at]
        second[lane].append(push(source, half.at[row], *sems, two))
        share(lane, source, row)

    def share(lane, source, row):
        if shares[lane]:
            at = 4 * depth - 1 + len(shared[lane])
            peer = {"replica": 1 - place.core}
            sems = sends.at[lane, at], recvs.at[lane, at]
            shared[lane].append(push(source, halves[lane].at[row], *sems, peer))

    keep = []
    for lane in lanes:
        own = halves[lane].at[place.me]
        keep.append(pltpu.make_async_copy(x_refs[lane], own, local.at[lane]))
        keep[lane].start()
        for step in range(1, depth):
            peer = {"fsdp": place.index(step, False, False)}
            sems = sends.at[lane, step - 1], recvs.at[lane, step - 1]
            line[lane].append(push(x_refs[lane], own, *sems, peer))
        pass_on(lane, x_refs[lane], 0, True)
    for step in range(1, depth):
        for lane in lanes:
            line[lane][step - 1].wait_recv()
            row = place.index(-step % depth, False, False)
            pass_on(lane, halves[lane].at[row], step, True)
    for number in range(depth):
        for lane in lanes:
            first[lane][number].wait_recv()
            row = place.index(-number % depth, True, False)
            pass_on(lane, halves[lane].at[row], number, False)
    for number in range(2 * depth):
        for lane in lanes:
            second[lane][number].wait_recv()
            row = place.index(-number % depth, number >= depth, True)
            share(lane, halves[lane].at[row], row)
    for lane in lanes:
        for copy in shared[lane]:
            copy.wait_recv()
        keep[lane].wait()
        for copy in line[lane] + first[lane] + second[lane] + shared[lane]:
            copy.wait_send()


def gathered(blocks, shares, number):
    group = lax.axis_size("fsdp")
    count = 2 * group - 1 if any(shares) else group - 1
    lanes = len(blocks)
    shapes = [
        jax.ShapeDtypeStruct(((2,) if share else ()) + (group,) + block.shape, block.dtype)
        for block, share in zip(blocks, shares)
    ]
    return pl.pallas_call(
        functools.partial(gather_kernel, group, shares),
        out_shape=shapes,
        in_specs=[pl.BlockSpec(memory_space=pl.ANY)] * lanes,
        out_specs=[pl.BlockSpec(memory_space=pl.ANY)] * lanes,
        scratch_shapes=[
            pltpu.SemaphoreType.DMA((lanes,)),
            pltpu.SemaphoreType.DMA((lanes, count)),
            pltpu.SemaphoreType.DMA((lanes, count)),
        ],
        compiler_params=pltpu.CompilerParams(collective_id=number, has_side_effects=True),
        cost_estimate=pl.CostEstimate(flops=0, bytes_accessed=150_000_000, transcendentals=0),
    )(*blocks)


def sum_kernel(group, count, small, *refs):
    inputs = count + (1 if small else 0)
    x_refs, outs = refs[:count], refs[inputs : inputs + count]
    got_one, got_two, got_line, to_two, to_line, sends, recvs = refs[2 * inputs : 2 * inputs + 7]
    place = Place(group)
    depth = place.depth
    meet(place, False)
    one = {"fsdp": place.index(0, True, False)}
    two = {"fsdp": place.index(0, False, True)}
    wide = jnp.float32
    lanes = range(count)
    first, second, line = [[[] for _ in lanes] for _ in range(3)]
    little = []
    if small:
        little_ref, little_out = refs[count], refs[inputs + count]
        hold, got, slots, little_sends, little_recvs = refs[2 * inputs + 7 :]
        sems = [(little_sends.at[i], little_recvs.at[i]) for i in range(depth + 1)]
        little.append(push(little_ref, got.at[0], *sems[0], one))
    for flip in (True, False):
        for lane in lanes:
            for step in range(depth):
                at = len(first[lane])
                block = x_refs[lane].at[place.index(step + 1, True, flip)]
                sem = sends.at[lane, at], recvs.at[lane, at]
                first[lane].append(push(block, got_one.at[lane, at], *sem, one))
    if small:
        little[0].wait_recv()
        hold[0] = little_ref[...] + got[0]
        little.append(push(hold.at[0], got.at[1], *sems[1], two))
    for lane in lanes:
        for step in range(depth):
            first[lane][step].wait_recv()
            total = x_refs[lane][place.index(step + 1, False, True)].astype(wide)
            total = total + got_one[lane, step].astype(wide)
            to_two[lane, step] = total.astype(to_two.dtype)
            at = 2 * depth + step
            sem = sends.at[lane, at], recvs.at[lane, at]
            second[lane].append(push(to_two.at[lane, step], got_two.at[lane, step], *sem, two))
    if small:
        little[1].wait_recv()
        hold[1] = hold[0] + got[1]
        slots[place.z] = hold[1]
        for step in range(1, depth):
            peer = {"fsdp": place.index(step, False, False)}
            little.append(push(hold.at[1], slots.at[place.z], *sems[step + 1], peer))
    for lane in lanes:
        for step in range(depth):
            first[lane][depth + step].wait_recv()
            second[lane][step].wait_recv()
            total = (
                x_refs[lane][place.index(step + 1, False, False)].astype(wide)
                + got_one[lane, depth + step].astype(wide)
                + got_two[lane, step].astype(wide)
            )
            if step < depth - 1:
                to_line[lane, step] = total.astype(to_line.dtype)
                at = 3 * depth + step
                sem = sends.at[lane, at], recvs.at[lane, at]
                peer = {"fsdp": place.index(step + 1, False, False)}
                line[lane].append(push(to_line.at[lane, step], got_line.at[lane, step], *sem, peer))
            else:
                outs[lane][...] = total
    for lane in lanes:
        for step in range(depth - 1):
            line[lane][step].wait_recv()
            outs[lane][...] += got_line[lane, step].astype(wide)
    if small:
        for copy in little[2:]:
            copy.wait_recv()
        total = slots[0]
        for step in range(1, depth):
            total = total + slots[step]
        little_out[...] = total
    for lane in lanes:
        for copy in first[lane] + second[lane] + line[lane]:
            copy.wait_send()
    for copy in little:
        copy.wait_send()


def sum_blocks(arrays, number, little=None):
    group = arrays[0].shape[0]
    depth = group // 4
    block = arrays[0].shape[1:]
    kind = arrays[0].dtype
    count = len(arrays)
    shapes = [jax.ShapeDtypeStruct(block, jnp.float32)] * count
    extra, scratch = [], []
    if little is not None:
        extra = [little]
        shapes = shapes + [jax.ShapeDtypeStruct(little.shape, jnp.float32)]
        scratch = [
            pltpu.VMEM((2,) + little.shape, jnp.float32),
            pltpu.VMEM((2,) + little.shape, jnp.float32),
            pltpu.VMEM((depth,) + little.shape, jnp.float32),
            pltpu.SemaphoreType.DMA((depth + 1,)),
            pltpu.SemaphoreType.DMA((depth + 1,)),
        ]
    return pl.pallas_call(
        functools.partial(sum_kernel, group, count, little is not None),
        out_shape=shapes,
        in_specs=[pl.BlockSpec(memory_space=pltpu.VMEM)] * len(shapes),
        out_specs=[pl.BlockSpec(memory_space=pltpu.VMEM)] * len(shapes),
        scratch_shapes=[
            pltpu.VMEM((count, 2 * depth) + block, kind),
            pltpu.VMEM((count, depth) + block, kind),
            pltpu.VMEM((count, depth - 1) + block, kind),
            pltpu.VMEM((count, depth) + block, kind),
            pltpu.VMEM((count, depth - 1) + block, kind),
            pltpu.SemaphoreType.DMA((count, group - 1)),
            pltpu.SemaphoreType.DMA((count, group - 1)),
        ]
        + scratch,
        compiler_params=pltpu.CompilerParams(
            collective_id=number, has_side_effects=True, vmem_limit_bytes=36 * 1024 * 1024
        ),
        cost_estimate=pl.CostEstimate(flops=0, bytes_accessed=150_000_000, transcendentals=0),
    )(*arrays, *extra)


def own_kernels():
    return lax.axis_size("fsdp") == 16 and lax.axis_size("replica") == 2


def gather_rows(block, number):
    if not own_kernels():
        return lax.all_gather(block, "fsdp", axis=0, tiled=True)
    return gathered([block], (False,), number)[0].reshape(-1, block.shape[1])


def other_core(value):
    return lax.ppermute(value, "replica", [(0, 1), (1, 0)])


def cores_sum(value):
    if lax.axis_size("replica") != 2:
        return lax.psum(value, "replica").astype(jnp.float32)
    return value.astype(jnp.float32) + other_core(value).astype(jnp.float32)


def mixer_sum(in_grad, out_grad, small):
    group = lax.axis_size("fsdp")
    both = jnp.concatenate([in_grad, out_grad], axis=1).astype(jnp.bfloat16)
    rows, columns = both.shape
    if not own_kernels():
        total = lax.psum_scatter(both, "fsdp", scatter_dimension=0, tiled=True)
        return cores_sum(total), lax.psum(small, ("fsdp", "replica"))
    core = lax.axis_index("replica")
    left, right = both[:, : columns // 2], both[:, columns // 2 :]
    mine = jnp.where(core == 0, left, right)
    theirs = other_core(jnp.where(core == 0, right, left))
    half = (mine.astype(jnp.float32) + theirs.astype(jnp.float32)).astype(jnp.bfloat16)
    little = jnp.pad(small, ((0, 8 - small.shape[0]), (0, 0)))
    half, little = sum_blocks([half.reshape(group, rows // group, columns // 2)], 5, little)
    little = (little + other_core(little))[: small.shape[0]]
    half = half.astype(jnp.bfloat16)
    back = other_core(half)
    whole = jnp.concatenate(
        [jnp.where(core == 0, half, back), jnp.where(core == 0, back, half)], axis=1
    )
    return whole.astype(jnp.float32), little


def passed_along(block, axis, distance):
    devices = range(lax.axis_size(axis))
    route = [(i - distance, i) for i in devices if i - distance in devices]
    return lax.ppermute(block, axis, route)


def rms_scale(v):
    return lax.rsqrt(jnp.mean(v * v, axis=-1, keepdims=True) + epsilon)


def product(left, right):
    return jnp.dot(left, right, preferred_element_type=jnp.float32)


def product_left(left, right):
    return lax.dot_general(
        left, right, (((0,), (0,)), ((), ())), preferred_element_type=jnp.float32
    )


def product_right(left, right):
    return lax.dot_general(
        left, right, (((1,), (1,)), ((), ())), preferred_element_type=jnp.float32
    )


def scattered_sums(values, number):
    values = [value.astype(jnp.bfloat16) for value in values]
    if not own_kernels():
        return [
            lax.psum_scatter(value, "fsdp", scatter_dimension=0, tiled=True).astype(jnp.float32)
            for value in values
        ]
    group = lax.axis_size("fsdp")
    return sum_blocks(
        [value.reshape(group, value.shape[0] // group, value.shape[1]) for value in values], number
    )


def norm_back(grad, scaled, scale, gain):
    grad_gain = grad * gain
    return scale * (grad_gain - scaled * jnp.mean(grad_gain * scaled, axis=-1, keepdims=True))


def body(
    tokens,
    cotangent,
    w_in,
    w_out,
    w_gate,
    w_up,
    w_down,
    norm1_scale,
    norm2_scale,
    conv_weight,
    dev_extra,
    seq_lengths,
):
    rows_dev = tokens.shape[0]
    width = tokens.shape[1]
    hidden = w_gate.shape[1]
    group = lax.axis_size("fsdp")
    part = w_down.shape[0]
    own_rows = w_gate.shape[0]
    pair = jnp.concatenate(
        [w_gate.reshape(own_rows, group, part), w_up.reshape(own_rows, group, part)], axis=2
    )
    pair = lax.all_to_all(
        pair.transpose(1, 0, 2), "fsdp", split_axis=0, concat_axis=0, tiled=True
    ).reshape(width, 2 * part)
    device = lax.axis_index(("fsdp", "replica"))
    counts = dev_extra + 2
    end_rows = jnp.cumsum(counts)
    device_ids = jnp.arange(counts.shape[0], dtype=jnp.int32)
    mine = device_ids == device
    count = jnp.sum(jnp.where(mine, counts, 0))
    offset = jnp.sum(jnp.where(mine, end_rows, 0)) - count
    row_ids = jnp.arange(rows_dev, dtype=jnp.int32)
    valid = row_ids < count
    position = offset + row_ids
    grad_out = jnp.where(valid[:, None], cotangent, jnp.zeros_like(cotangent))
    if own_kernels():
        late = jnp.concatenate([w_in[:, 2 * width :], w_out], axis=1)
        chosen = jnp.where(lax.axis_index("replica") == 0, w_in[:, : 2 * width], late)
        halves, grad_all = gathered([chosen, grad_out], (True, False), 0)
        halves = halves.reshape(2, width, 2 * width)
        grad_all = grad_all.reshape(-1, width)
        whole_bc, whole_x, whole_out = halves[0], halves[1, :, :width], halves[1, :, width:]
    else:
        whole_in = lax.all_gather(w_in, "fsdp", axis=0, tiled=True)
        whole_bc, whole_x = whole_in[:, : 2 * width], whole_in[:, 2 * width :]
        whole_out = lax.all_gather(w_out, "fsdp", axis=0, tiled=True)
        grad_all = lax.all_gather(grad_out, "fsdp", axis=0, tiled=True)
    seq_first = jnp.cumsum(seq_lengths) - seq_lengths
    is_start = jnp.any(position[:, None] == seq_first[None, :], axis=1)
    prev_start = jnp.any((position - 1)[:, None] == seq_first[None, :], axis=1)
    keep_one = (valid & jnp.logical_not(is_start)).astype(jnp.float32)[:, None]
    keep_two = keep_one * jnp.logical_not(prev_start).astype(jnp.float32)[:, None]
    inputs = tokens.astype(jnp.float32)
    scale_one = rms_scale(inputs)
    scaled_one = inputs * scale_one
    normed_in = (scaled_one * norm1_scale).astype(jnp.bfloat16)
    bc_part = product(normed_in, whole_bc).astype(jnp.bfloat16)
    b_part = bc_part[:, :width]
    c_part = bc_part[:, width:]
    x_part = product(normed_in, whole_x).astype(jnp.bfloat16)
    rim_pair = (
        lax.dynamic_slice_in_dim(b_part, count - 2, 2, 0),
        lax.dynamic_slice_in_dim(x_part, count - 2, 2, 0),
    )
    rim = passed_along(jnp.concatenate(rim_pair, axis=0), ("fsdp", "replica"), 1)
    rim_b, rim_x = rim[:2], rim[2:]
    b_val = b_part.astype(jnp.float32)
    x_val = x_part.astype(jnp.float32)
    c_val = c_part.astype(jnp.float32)
    u = b_val * x_val
    u_ext = jnp.concatenate([rim_b.astype(jnp.float32) * rim_x.astype(jnp.float32), u], axis=0)
    u_prev = u_ext[1 : rows_dev + 1] * keep_one
    u_prev2 = u_ext[:rows_dev] * keep_two
    v = conv_weight[2] * u + conv_weight[1] * u_prev + conv_weight[0] * u_prev2
    y_val = (c_val * v).astype(jnp.bfloat16)
    hidden_res = inputs + product(y_val, whole_out)
    scale_two = rms_scale(hidden_res)
    scaled_two = hidden_res * scale_two
    normed_ffn = (scaled_two * norm2_scale).astype(jnp.bfloat16)
    ffn_all = gather_rows(normed_ffn, 2)
    both = product(ffn_all, pair)
    gate_val, up_val = both[:, :part], both[:, part:]
    sigma = jax.nn.sigmoid(gate_val)
    silu_val = gate_val * sigma
    act_val = (silu_val * up_val).astype(jnp.bfloat16)
    grad_act = product_right(grad_all, w_down)
    grad_gate = (grad_act * up_val * sigma * (1.0 + gate_val * (1.0 - sigma))).astype(jnp.bfloat16)
    grad_up = (grad_act * silu_val).astype(jnp.bfloat16)
    grad_pair = jnp.concatenate([grad_gate, grad_up], axis=1)
    grad_ffn, down_sum = scattered_sums(
        [product_right(grad_pair, pair), product(act_val, w_down)], 3
    )
    result = hidden_res + down_sum
    block_out = jnp.where(valid[:, None], result, 0.0).astype(jnp.bfloat16)
    gain_two = jnp.sum(grad_ffn * scaled_two, axis=0)
    grad_res = grad_out.astype(jnp.float32) + norm_back(
        grad_ffn, scaled_two, scale_two, norm2_scale
    )
    grad_mix = grad_res.astype(jnp.bfloat16)
    grad_y = product_right(grad_mix, whole_out)
    grad_c = grad_y * v
    grad_v = grad_y * c_val
    conv_grads = jnp.stack(
        [
            jnp.sum(grad_v * u_prev2, axis=0),
            jnp.sum(grad_v * u_prev, axis=0),
            jnp.sum(grad_v * u, axis=0),
        ]
    )
    term_one = conv_weight[1] * keep_one * grad_v
    term_two = conv_weight[0] * keep_two * grad_v
    grad_ext = (
        jnp.pad(term_two, ((0, 2), (0, 0)))
        + jnp.pad(term_one, ((1, 1), (0, 0)))
        + jnp.pad(conv_weight[2] * grad_v, ((2, 0), (0, 0)))
    )
    from_next = passed_along(grad_ext[:2], ("fsdp", "replica"), -1)
    grad_u = grad_ext[2:]
    grad_u = grad_u + lax.dynamic_update_slice_in_dim(
        jnp.zeros_like(grad_u), from_next, count - 2, 0
    )
    grad_proj = jnp.concatenate([grad_u * x_val, grad_c, grad_u * b_val], axis=1).astype(
        jnp.bfloat16
    )
    grad_norm_in = product_right(grad_proj[:, : 2 * width], whole_bc) + product_right(
        grad_proj[:, 2 * width :], whole_x
    )
    gain_one = jnp.sum(grad_norm_in * scaled_one, axis=0)
    d_tokens = (grad_res + norm_back(grad_norm_in, scaled_one, scale_one, norm1_scale)).astype(
        jnp.bfloat16
    )
    mix_part, small = mixer_sum(
        product_left(normed_in, grad_proj),
        product_left(y_val, grad_mix),
        jnp.concatenate([gain_one[None], gain_two[None], conv_grads], axis=0),
    )
    d_norm1, d_norm2, d_conv = small[0], small[1], small[2:]
    pair_part = product_left(ffn_all, grad_pair).astype(jnp.bfloat16)
    pair_part = lax.all_to_all(
        pair_part.reshape(group, own_rows, 2 * part), "fsdp", split_axis=0, concat_axis=0, tiled=True
    )
    down_part = product_left(act_val, grad_all)
    pair_part = cores_sum(pair_part)
    down_part = cores_sum(down_part.astype(jnp.bfloat16))
    d_w_in = mix_part[:, : 3 * width]
    d_w_out = mix_part[:, 3 * width :]
    pair_part = pair_part.transpose(1, 0, 2)
    d_w_gate = pair_part[:, :, :part].reshape(own_rows, hidden)
    d_w_up = pair_part[:, :, part:].reshape(own_rows, hidden)
    return (
        block_out,
        d_tokens,
        d_w_in,
        d_w_out,
        d_w_gate,
        d_w_up,
        down_part,
        d_norm1,
        d_norm2,
        d_conv,
    )


def solution(mesh):
    placed = (
        P(("fsdp", "replica"), None),
        P(("fsdp", "replica"), None),
        P("fsdp", None),
        P("fsdp", None),
        P("fsdp", None),
        P("fsdp", None),
        P("fsdp", None),
        P(),
        P(),
        P(),
        P(),
        P(),
    )
    return jax.shard_map(
        body,
        mesh=mesh,
        in_specs=placed,
        out_specs=(
            P(("fsdp", "replica"), None),
            P(("fsdp", "replica"), None),
            P("fsdp", None),
            P("fsdp", None),
            P("fsdp", None),
            P("fsdp", None),
            P("fsdp", None),
            P(),
            P(),
            P(),
        ),
        check_vma=False,
    )
```

```python
import functools

import jax
import jax.numpy as jnp
from jax import lax
from jax.experimental import pallas as pl
from jax.experimental.pallas import tpu as pltpu
from jax.sharding import PartitionSpec as P

epsilon = 1e-05


class Place:
    def __init__(self, group):
        self.me = lax.axis_index("fsdp")
        self.core = lax.axis_index("replica")
        self.depth = group // 4
        self.mask_one = 1 + self.core
        self.mask_two = 2 - self.core
        self.bit_one = lax.rem(lax.div(self.me, self.mask_one), 2)
        self.bit_two = lax.rem(lax.div(self.me, self.mask_two), 2)
        self.z = lax.div(self.me, 4)

    def index(self, step, flip_one, flip_two):
        z = lax.rem(self.z + step, self.depth)
        one = 1 - self.bit_one if flip_one else self.bit_one
        two = 1 - self.bit_two if flip_two else self.bit_two
        return 4 * z + self.mask_one * one + self.mask_two * two

    def peers(self):
        line = [self.index(step, False, False) for step in range(1, self.depth)]
        return line + [self.index(0, True, False), self.index(0, False, True)]


def meet(place, sibling):
    barrier = pltpu.get_barrier_semaphore()
    peers = [{"fsdp": peer} for peer in place.peers()]
    if sibling:
        peers.append({"replica": 1 - place.core})
    for peer in peers:
        pl.semaphore_signal(barrier, inc=1, device_id=peer, device_id_type=pl.DeviceIdType.MESH)
    pl.semaphore_wait(barrier, len(peers))


def push(source, target, send, recv, peer):
    copy = pltpu.make_async_remote_copy(
        src_ref=source,
        dst_ref=target,
        send_sem=send,
        recv_sem=recv,
        device_id=peer,
        device_id_type=pl.DeviceIdType.MESH,
    )
    copy.start()
    return copy


def gather_kernel(group, shares, *refs):
    count = len(shares)
    x_refs, outs = refs[:count], refs[count : 2 * count]
    local, sends, recvs = refs[2 * count :]
    place = Place(group)
    depth = place.depth
    meet(place, any(shares))
    halves = [out.at[place.core] if share else out for out, share in zip(outs, shares)]
    one = {"fsdp": place.index(0, True, False)}
    two = {"fsdp": place.index(0, False, True)}
    lanes = range(count)
    line, first, second, shared = [[[] for _ in lanes] for _ in range(4)]

    def pass_on(lane, source, number, to_one):
        half = halves[lane]
        row = place.index(-number % depth, not to_one, False)
        if to_one:
            at = depth - 1 + number
            sems = sends.at[lane, at], recvs.at[lane, at]
            first[lane].append(push(source, half.at[row], *sems, one))
        at = 2 * depth - 1 + len(second[lane])
        sems = sends.at[lane, at], recvs.at[lane, at]
        second[lane].append(push(source, half.at[row], *sems, two))
        share(lane, source, row)

    def share(lane, source, row):
        if shares[lane]:
            at = 4 * depth - 1 + len(shared[lane])
            peer = {"replica": 1 - place.core}
            sems = sends.at[lane, at], recvs.at[lane, at]
            shared[lane].append(push(source, halves[lane].at[row], *sems, peer))

    keep = []
    for lane in lanes:
        own = halves[lane].at[place.me]
        keep.append(pltpu.make_async_copy(x_refs[lane], own, local.at[lane]))
        keep[lane].start()
        for step in range(1, depth):
            peer = {"fsdp": place.index(step, False, False)}
            sems = sends.at[lane, step - 1], recvs.at[lane, step - 1]
            line[lane].append(push(x_refs[lane], own, *sems, peer))
        pass_on(lane, x_refs[lane], 0, True)
    for step in range(1, depth):
        for lane in lanes:
            line[lane][step - 1].wait_recv()
            row = place.index(-step % depth, False, False)
            pass_on(lane, halves[lane].at[row], step, True)
    for number in range(depth):
        for lane in lanes:
            first[lane][number].wait_recv()
            row = place.index(-number % depth, True, False)
            pass_on(lane, halves[lane].at[row], number, False)
    for number in range(2 * depth):
        for lane in lanes:
            second[lane][number].wait_recv()
            row = place.index(-number % depth, number >= depth, True)
            share(lane, halves[lane].at[row], row)
    for lane in lanes:
        for copy in shared[lane]:
            copy.wait_recv()
        keep[lane].wait()
        for copy in line[lane] + first[lane] + second[lane] + shared[lane]:
            copy.wait_send()


def gathered(blocks, shares, number):
    group = lax.axis_size("fsdp")
    count = 2 * group - 1 if any(shares) else group - 1
    lanes = len(blocks)
    shapes = [
        jax.ShapeDtypeStruct(((2,) if share else ()) + (group,) + block.shape, block.dtype)
        for block, share in zip(blocks, shares)
    ]
    return pl.pallas_call(
        functools.partial(gather_kernel, group, shares),
        out_shape=shapes,
        in_specs=[pl.BlockSpec(memory_space=pl.ANY)] * lanes,
        out_specs=[pl.BlockSpec(memory_space=pl.ANY)] * lanes,
        scratch_shapes=[
            pltpu.SemaphoreType.DMA((lanes,)),
            pltpu.SemaphoreType.DMA((lanes, count)),
            pltpu.SemaphoreType.DMA((lanes, count)),
        ],
        compiler_params=pltpu.CompilerParams(collective_id=number, has_side_effects=True),
        cost_estimate=pl.CostEstimate(flops=0, bytes_accessed=150_000_000, transcendentals=0),
    )(*blocks)


def sum_kernel(group, count, small, *refs):
    inputs = count + (1 if small else 0)
    x_refs, outs = refs[:count], refs[inputs : inputs + count]
    got_one, got_two, got_line, to_two, to_line, sends, recvs = refs[2 * inputs : 2 * inputs + 7]
    place = Place(group)
    depth = place.depth
    meet(place, False)
    one = {"fsdp": place.index(0, True, False)}
    two = {"fsdp": place.index(0, False, True)}
    wide = jnp.float32
    lanes = range(count)
    first, second, line = [[[] for _ in lanes] for _ in range(3)]
    little = []
    if small:
        little_ref, little_out = refs[count], refs[inputs + count]
        hold, got, slots, little_sends, little_recvs = refs[2 * inputs + 7 :]
        sems = [(little_sends.at[i], little_recvs.at[i]) for i in range(depth + 1)]
        little.append(push(little_ref, got.at[0], *sems[0], one))
    for flip in (True, False):
        for lane in lanes:
            for step in range(depth):
                at = len(first[lane])
                block = x_refs[lane].at[place.index(step + 1, True, flip)]
                sem = sends.at[lane, at], recvs.at[lane, at]
                first[lane].append(push(block, got_one.at[lane, at], *sem, one))
    if small:
        little[0].wait_recv()
        hold[0] = little_ref[...] + got[0]
        little.append(push(hold.at[0], got.at[1], *sems[1], two))
    for lane in lanes:
        for step in range(depth):
            first[lane][step].wait_recv()
            total = x_refs[lane][place.index(step + 1, False, True)].astype(wide)
            total = total + got_one[lane, step].astype(wide)
            to_two[lane, step] = total.astype(to_two.dtype)
            at = 2 * depth + step
            sem = sends.at[lane, at], recvs.at[lane, at]
            second[lane].append(push(to_two.at[lane, step], got_two.at[lane, step], *sem, two))
    if small:
        little[1].wait_recv()
        hold[1] = hold[0] + got[1]
        slots[place.z] = hold[1]
        for step in range(1, depth):
            peer = {"fsdp": place.index(step, False, False)}
            little.append(push(hold.at[1], slots.at[place.z], *sems[step + 1], peer))
    for lane in lanes:
        for step in range(depth):
            first[lane][depth + step].wait_recv()
            second[lane][step].wait_recv()
            total = (
                x_refs[lane][place.index(step + 1, False, False)].astype(wide)
                + got_one[lane, depth + step].astype(wide)
                + got_two[lane, step].astype(wide)
            )
            if step < depth - 1:
                to_line[lane, step] = total.astype(to_line.dtype)
                at = 3 * depth + step
                sem = sends.at[lane, at], recvs.at[lane, at]
                peer = {"fsdp": place.index(step + 1, False, False)}
                line[lane].append(push(to_line.at[lane, step], got_line.at[lane, step], *sem, peer))
            else:
                outs[lane][...] = total
    for lane in lanes:
        for step in range(depth - 1):
            line[lane][step].wait_recv()
            outs[lane][...] += got_line[lane, step].astype(wide)
    if small:
        for copy in little[2:]:
            copy.wait_recv()
        total = slots[0]
        for step in range(1, depth):
            total = total + slots[step]
        little_out[...] = total
    for lane in lanes:
        for copy in first[lane] + second[lane] + line[lane]:
            copy.wait_send()
    for copy in little:
        copy.wait_send()


def sum_blocks(arrays, number, little=None):
    group = arrays[0].shape[0]
    depth = group // 4
    block = arrays[0].shape[1:]
    kind = arrays[0].dtype
    count = len(arrays)
    shapes = [jax.ShapeDtypeStruct(block, jnp.float32)] * count
    extra, scratch = [], []
    if little is not None:
        extra = [little]
        shapes = shapes + [jax.ShapeDtypeStruct(little.shape, jnp.float32)]
        scratch = [
            pltpu.VMEM((2,) + little.shape, jnp.float32),
            pltpu.VMEM((2,) + little.shape, jnp.float32),
            pltpu.VMEM((depth,) + little.shape, jnp.float32),
            pltpu.SemaphoreType.DMA((depth + 1,)),
            pltpu.SemaphoreType.DMA((depth + 1,)),
        ]
    return pl.pallas_call(
        functools.partial(sum_kernel, group, count, little is not None),
        out_shape=shapes,
        in_specs=[pl.BlockSpec(memory_space=pltpu.VMEM)] * len(shapes),
        out_specs=[pl.BlockSpec(memory_space=pltpu.VMEM)] * len(shapes),
        scratch_shapes=[
            pltpu.VMEM((count, 2 * depth) + block, kind),
            pltpu.VMEM((count, depth) + block, kind),
            pltpu.VMEM((count, depth - 1) + block, kind),
            pltpu.VMEM((count, depth) + block, kind),
            pltpu.VMEM((count, depth - 1) + block, kind),
            pltpu.SemaphoreType.DMA((count, group - 1)),
            pltpu.SemaphoreType.DMA((count, group - 1)),
        ]
        + scratch,
        compiler_params=pltpu.CompilerParams(
            collective_id=number, has_side_effects=True, vmem_limit_bytes=36 * 1024 * 1024
        ),
        cost_estimate=pl.CostEstimate(flops=0, bytes_accessed=150_000_000, transcendentals=0),
    )(*arrays, *extra)


def own_kernels():
    return lax.axis_size("fsdp") == 16 and lax.axis_size("replica") == 2


def gather_rows(block, number):
    if not own_kernels():
        return lax.all_gather(block, "fsdp", axis=0, tiled=True)
    return gathered([block], (False,), number)[0].reshape(-1, block.shape[1])


def other_core(value):
    return lax.ppermute(value, "replica", [(0, 1), (1, 0)])


def cores_sum(value):
    if lax.axis_size("replica") != 2:
        return lax.psum(value, "replica").astype(jnp.float32)
    return value.astype(jnp.float32) + other_core(value).astype(jnp.float32)


def mixer_sum(in_grad, out_grad, small):
    group = lax.axis_size("fsdp")
    both = jnp.concatenate([in_grad, out_grad], axis=1).astype(jnp.bfloat16)
    rows, columns = both.shape
    if not own_kernels():
        total = lax.psum_scatter(both, "fsdp", scatter_dimension=0, tiled=True)
        return cores_sum(total), lax.psum(small, ("fsdp", "replica"))
    core = lax.axis_index("replica")
    left, right = both[:, : columns // 2], both[:, columns // 2 :]
    mine = jnp.where(core == 0, left, right)
    theirs = other_core(jnp.where(core == 0, right, left))
    half = (mine.astype(jnp.float32) + theirs.astype(jnp.float32)).astype(jnp.bfloat16)
    little = jnp.pad(small, ((0, 8 - small.shape[0]), (0, 0)))
    half, little = sum_blocks([half.reshape(group, rows // group, columns // 2)], 5, little)
    little = (little + other_core(little))[: small.shape[0]]
    half = half.astype(jnp.bfloat16)
    back = other_core(half)
    whole = jnp.concatenate(
        [jnp.where(core == 0, half, back), jnp.where(core == 0, back, half)], axis=1
    )
    return whole.astype(jnp.float32), little


def passed_along(block, axis, distance):
    devices = range(lax.axis_size(axis))
    route = [(i - distance, i) for i in devices if i - distance in devices]
    return lax.ppermute(block, axis, route)


def rms_scale(v):
    return lax.rsqrt(jnp.mean(v * v, axis=-1, keepdims=True) + epsilon)


def product(left, right):
    return jnp.dot(left, right, preferred_element_type=jnp.float32)


def product_left(left, right):
    return lax.dot_general(
        left, right, (((0,), (0,)), ((), ())), preferred_element_type=jnp.float32
    )


def product_right(left, right):
    return lax.dot_general(
        left, right, (((1,), (1,)), ((), ())), preferred_element_type=jnp.float32
    )


def scattered_sums(values, number):
    values = [value.astype(jnp.bfloat16) for value in values]
    if not own_kernels():
        return [
            lax.psum_scatter(value, "fsdp", scatter_dimension=0, tiled=True).astype(jnp.float32)
            for value in values
        ]
    group = lax.axis_size("fsdp")
    return sum_blocks(
        [value.reshape(group, value.shape[0] // group, value.shape[1]) for value in values], number
    )


def norm_back(grad, scaled, scale, gain):
    grad_gain = grad * gain
    return scale * (grad_gain - scaled * jnp.mean(grad_gain * scaled, axis=-1, keepdims=True))


def body(
    tokens,
    cotangent,
    w_in,
    w_out,
    w_gate,
    w_up,
    w_down,
    norm1_scale,
    norm2_scale,
    conv_weight,
    dev_extra,
    seq_lengths,
):
    rows_dev = tokens.shape[0]
    width = tokens.shape[1]
    hidden = w_gate.shape[1]
    group = lax.axis_size("fsdp")
    part = w_down.shape[0]
    own_rows = w_gate.shape[0]
    pair = jnp.concatenate(
        [w_gate.reshape(own_rows, group, part), w_up.reshape(own_rows, group, part)], axis=2
    )
    pair = lax.all_to_all(
        pair.transpose(1, 0, 2), "fsdp", split_axis=0, concat_axis=0, tiled=True
    ).reshape(width, 2 * part)
    device = lax.axis_index(("fsdp", "replica"))
    counts = dev_extra + 2
    end_rows = jnp.cumsum(counts)
    device_ids = jnp.arange(counts.shape[0], dtype=jnp.int32)
    mine = device_ids == device
    count = jnp.sum(jnp.where(mine, counts, 0))
    offset = jnp.sum(jnp.where(mine, end_rows, 0)) - count
    row_ids = jnp.arange(rows_dev, dtype=jnp.int32)
    valid = row_ids < count
    position = offset + row_ids
    grad_out = jnp.where(valid[:, None], cotangent, jnp.zeros_like(cotangent))
    if own_kernels():
        late = jnp.concatenate([w_in[:, 2 * width :], w_out], axis=1)
        chosen = jnp.where(lax.axis_index("replica") == 0, w_in[:, : 2 * width], late)
        halves, grad_all = gathered([chosen, grad_out], (True, False), 0)
        halves = halves.reshape(2, width, 2 * width)
        grad_all = grad_all.reshape(-1, width)
        whole_bc, whole_x, whole_out = halves[0], halves[1, :, :width], halves[1, :, width:]
    else:
        whole_in = lax.all_gather(w_in, "fsdp", axis=0, tiled=True)
        whole_bc, whole_x = whole_in[:, : 2 * width], whole_in[:, 2 * width :]
        whole_out = lax.all_gather(w_out, "fsdp", axis=0, tiled=True)
        grad_all = lax.all_gather(grad_out, "fsdp", axis=0, tiled=True)
    seq_first = jnp.cumsum(seq_lengths) - seq_lengths
    is_start = jnp.any(position[:, None] == seq_first[None, :], axis=1)
    prev_start = jnp.any((position - 1)[:, None] == seq_first[None, :], axis=1)
    keep_one = (valid & jnp.logical_not(is_start)).astype(jnp.float32)[:, None]
    keep_two = keep_one * jnp.logical_not(prev_start).astype(jnp.float32)[:, None]
    inputs = tokens.astype(jnp.float32)
    scale_one = rms_scale(inputs)
    scaled_one = inputs * scale_one
    normed_in = (scaled_one * norm1_scale).astype(jnp.bfloat16)
    bc_part = product(normed_in, whole_bc).astype(jnp.bfloat16)
    b_part = bc_part[:, :width]
    c_part = bc_part[:, width:]
    x_part = product(normed_in, whole_x).astype(jnp.bfloat16)
    rim_pair = (
        lax.dynamic_slice_in_dim(b_part, count - 2, 2, 0),
        lax.dynamic_slice_in_dim(x_part, count - 2, 2, 0),
    )
    rim = passed_along(jnp.concatenate(rim_pair, axis=0), ("fsdp", "replica"), 1)
    rim_b, rim_x = rim[:2], rim[2:]
    b_val = b_part.astype(jnp.float32)
    x_val = x_part.astype(jnp.float32)
    c_val = c_part.astype(jnp.float32)
    u = b_val * x_val
    u_ext = jnp.concatenate([rim_b.astype(jnp.float32) * rim_x.astype(jnp.float32), u], axis=0)
    u_prev = u_ext[1 : rows_dev + 1] * keep_one
    u_prev2 = u_ext[:rows_dev] * keep_two
    v = conv_weight[2] * u + conv_weight[1] * u_prev + conv_weight[0] * u_prev2
    y_val = (c_val * v).astype(jnp.bfloat16)
    hidden_res = inputs + product(y_val, whole_out)
    scale_two = rms_scale(hidden_res)
    scaled_two = hidden_res * scale_two
    normed_ffn = (scaled_two * norm2_scale).astype(jnp.bfloat16)
    ffn_all = gather_rows(normed_ffn, 2)
    both = product(ffn_all, pair)
    gate_val, up_val = both[:, :part], both[:, part:]
    sigma = jax.nn.sigmoid(gate_val)
    silu_val = gate_val * sigma
    act_val = (silu_val * up_val).astype(jnp.bfloat16)
    grad_act = product_right(grad_all, w_down)
    grad_gate = (grad_act * up_val * sigma * (1.0 + gate_val * (1.0 - sigma))).astype(jnp.bfloat16)
    grad_up = (grad_act * silu_val).astype(jnp.bfloat16)
    grad_pair = jnp.concatenate([grad_gate, grad_up], axis=1)
    pair_part = product_left(ffn_all, grad_pair).astype(jnp.bfloat16)
    pair_part, grad_pair = lax.optimization_barrier((pair_part, grad_pair))
    pair_part = lax.all_to_all(
        pair_part.reshape(group, own_rows, 2 * part), "fsdp", split_axis=0, concat_axis=0, tiled=True
    )
    grad_ffn, down_sum = scattered_sums(
        [product_right(grad_pair, pair), product(act_val, w_down)], 3
    )
    pair_part, grad_ffn = lax.optimization_barrier((pair_part, grad_ffn))
    result = hidden_res + down_sum
    block_out = jnp.where(valid[:, None], result, 0.0).astype(jnp.bfloat16)
    gain_two = jnp.sum(grad_ffn * scaled_two, axis=0)
    grad_res = grad_out.astype(jnp.float32) + norm_back(
        grad_ffn, scaled_two, scale_two, norm2_scale
    )
    grad_mix = grad_res.astype(jnp.bfloat16)
    grad_y = product_right(grad_mix, whole_out)
    grad_c = grad_y * v
    grad_v = grad_y * c_val
    conv_grads = jnp.stack(
        [
            jnp.sum(grad_v * u_prev2, axis=0),
            jnp.sum(grad_v * u_prev, axis=0),
            jnp.sum(grad_v * u, axis=0),
        ]
    )
    term_one = conv_weight[1] * keep_one * grad_v
    term_two = conv_weight[0] * keep_two * grad_v
    grad_ext = (
        jnp.pad(term_two, ((0, 2), (0, 0)))
        + jnp.pad(term_one, ((1, 1), (0, 0)))
        + jnp.pad(conv_weight[2] * grad_v, ((2, 0), (0, 0)))
    )
    from_next = passed_along(grad_ext[:2], ("fsdp", "replica"), -1)
    grad_u = grad_ext[2:]
    grad_u = grad_u + lax.dynamic_update_slice_in_dim(
        jnp.zeros_like(grad_u), from_next, count - 2, 0
    )
    grad_proj = jnp.concatenate([grad_u * x_val, grad_c, grad_u * b_val], axis=1).astype(
        jnp.bfloat16
    )
    grad_norm_in = product_right(grad_proj[:, : 2 * width], whole_bc) + product_right(
        grad_proj[:, 2 * width :], whole_x
    )
    gain_one = jnp.sum(grad_norm_in * scaled_one, axis=0)
    d_tokens = (grad_res + norm_back(grad_norm_in, scaled_one, scale_one, norm1_scale)).astype(
        jnp.bfloat16
    )
    mix_part, small = mixer_sum(
        product_left(normed_in, grad_proj),
        product_left(y_val, grad_mix),
        jnp.concatenate([gain_one[None], gain_two[None], conv_grads], axis=0),
    )
    d_norm1, d_norm2, d_conv = small[0], small[1], small[2:]
    down_part = product_left(act_val, grad_all)
    pair_part = cores_sum(pair_part)
    down_part = cores_sum(down_part.astype(jnp.bfloat16))
    d_w_in = mix_part[:, : 3 * width]
    d_w_out = mix_part[:, 3 * width :]
    pair_part = pair_part.transpose(1, 0, 2)
    d_w_gate = pair_part[:, :, :part].reshape(own_rows, hidden)
    d_w_up = pair_part[:, :, part:].reshape(own_rows, hidden)
    return (
        block_out,
        d_tokens,
        d_w_in,
        d_w_out,
        d_w_gate,
        d_w_up,
        down_part,
        d_norm1,
        d_norm2,
        d_conv,
    )


def solution(mesh):
    placed = (
        P(("fsdp", "replica"), None),
        P(("fsdp", "replica"), None),
        P("fsdp", None),
        P("fsdp", None),
        P("fsdp", None),
        P("fsdp", None),
        P("fsdp", None),
        P(),
        P(),
        P(),
        P(),
        P(),
    )
    return jax.shard_map(
        body,
        mesh=mesh,
        in_specs=placed,
        out_specs=(
            P(("fsdp", "replica"), None),
            P(("fsdp", "replica"), None),
            P("fsdp", None),
            P("fsdp", None),
            P("fsdp", None),
            P("fsdp", None),
            P("fsdp", None),
            P(),
            P(),
            P(),
        ),
        check_vma=False,
    )
```
